32 devices in a mesh: groups: 2 (over y), ctx: 4 (over z), dp: 2 (over x), mp: 2 (over core).
Axes of the slice: x: 2, y: 2, z: 4, core: 2. Of those that a mesh axis runs over, the one named last changes fastest.
Arguments:
- head_inputs: bfloat16 [3, 4, 1024, 1536], P(None, ('groups', 'dp'), 'ctx', 'mp'), parts along dimension 1, may hold values from -0.29882812 to 0.29882812
- write_read: bfloat16 [3, 4, 1024, 128], P(None, ('groups', 'dp'), 'ctx'), parts along dimension 1, may hold values from -0.26953125 to 0.26953125
- decay_steps: int32 [3, 4, 12, 1024], P(None, ('groups', 'dp'), 'mp', 'ctx'), parts along dimension 1, may hold values from 0 to 512
- scan_orders: int32 [2, 4, 1024], P(None, ('groups', 'dp'), 'ctx'), parts along dimension 1, may hold values from 0 to 1023, as said below
- cotangent: bfloat16 [4, 1024, 768], P(('groups', 'dp'), 'ctx'), parts along dimension 0, may hold values from -0.59765625 to 0.59765625
- out_weight: bfloat16 [3, 768, 1536], P(None, 'ctx', 'mp'), may hold values from -0.4375 to 0.4375
Outputs:
- grad_inputs: bfloat16 [3, 4, 1024, 1536], P(None, ('groups', 'dp'), 'ctx', 'mp'), parts along dimension 1
- grad_write_read: bfloat16 [3, 4, 1024, 128], P(None, ('groups', 'dp'), 'ctx'), parts along dimension 1
- grad_weight: bfloat16 [6, 768, 1536], P('groups', 'ctx', 'mp'), parts along dimension 0
The draws below stay inside these ranges and needn't reach their ends.
There are 2 independent parts, one for each index of `groups`. The reference program is written for one: setup_inputs(seed, part) draws one part's arguments, and reference() takes and returns one part's arrays. A program takes and returns all parts, laid end to end along the dimension named above; an argument that names none is the same for every part. Nothing has to cross between parts.
Inputs may be any that keep to these rules, and one draw needn't show every extreme that they name: `scan_orders`: for every volume and each of the two orders, position d * 256 + q * 64 + m (0 <= m < 64) holds a patch of index q * 256 + d * 64 + m' with 0 <= m' < 64; every patch stands at exactly one position.
All inputs are finite; a program needn't handle non-finite values.
Results may differ from the reference program's by a relative error of at most 0.005.
Values may be sent and summed in bfloat16 or wider, within the bound.
A program may use at most 128 MiB of HBM per device.

```python
import math
import jax
import jax.numpy as jnp
from jax import lax

D = 768
ATTENTION_SPLITS = 12
P_SIZE = 128
N = 64
TOK_DEV = 256
SCAN_SAMPLES = 2
PIECE_ELEMENTS = 1024
BLOCK = 64


def draw_decay_steps(key, part):
    stochastic_seeds = jax.random.split(key, 5)
    blocks = PIECE_ELEMENTS // TOK_DEV
    slow_heads = jax.random.randint(stochastic_seeds[0], (3, SCAN_SAMPLES, ATTENTION_SPLITS, 1), 0, 2)
    factor = jax.random.randint(stochastic_seeds[1], (3, SCAN_SAMPLES, ATTENTION_SPLITS, blocks, 1), 1, 3)
    slow_rates = (jax.random.randint(stochastic_seeds[2], (3, SCAN_SAMPLES, ATTENTION_SPLITS, blocks, TOK_DEV), 0, 2) * factor).reshape(3, SCAN_SAMPLES, ATTENTION_SPLITS, PIECE_ELEMENTS)
    fast_rates = jax.random.randint(stochastic_seeds[3], (3, SCAN_SAMPLES, ATTENTION_SPLITS, PIECE_ELEMENTS), PIECE_ELEMENTS // 40, PIECE_ELEMENTS // 15 + 1)
    baseline = jnp.where(slow_heads == 1, slow_rates, fast_rates)
    cluster_sets = jax.random.randint(stochastic_seeds[4], (3, SCAN_SAMPLES, ATTENTION_SPLITS, 2, 1), 0, PIECE_ELEMENTS)
    location_numbers = jnp.arange(PIECE_ELEMENTS, dtype=jnp.int32)
    dropped_lines = jnp.any(cluster_sets == location_numbers, axis=3)
    return jnp.where(dropped_lines, PIECE_ELEMENTS // 2, baseline).astype(jnp.int32)


def draw_scan_orders(key, part):
    ctx_count = TOK_DEV // BLOCK
    within = jnp.broadcast_to(jnp.arange(BLOCK, dtype=jnp.int32), (2, SCAN_SAMPLES, ctx_count, ctx_count, BLOCK))
    mixed = jax.random.permutation(key, within, axis=4, independent=True)
    target = jnp.arange(ctx_count, dtype=jnp.int32)[:, None, None]
    source = jnp.arange(ctx_count, dtype=jnp.int32)[None, :, None]
    patches = source * TOK_DEV + target * BLOCK + mixed
    return patches.reshape(2, SCAN_SAMPLES, PIECE_ELEMENTS).astype(jnp.int32)


def strengthened(values, key, source, target, shards_of, factor):
    owner, partner = [(jnp.arange(values.shape[position]) // (values.shape[position] // shards_of)).reshape([-1 if axis == position else 1 for axis in range(values.ndim)]) for position in (source, target)]
    chosen = jax.random.permutation(key, shards_of)[partner]
    strong = (owner == chosen) | (owner == (partner + shards_of // 2) % shards_of)
    return jnp.where(strong, factor * values, values)


def shard_levels(own_key, dims, cuts, low, high):
    def one(axis_at, parts):
        draws = jax.random.uniform(jax.random.fold_in(jax.random.fold_in(own_key, 6), axis_at), (parts,), jnp.float32, low / len(cuts), high / len(cuts))
        return jnp.repeat(jnp.exp(draws), dims[axis_at] // parts).reshape((-1,) + (1,) * (len(dims) - axis_at - 1))

    loudness = one(*cuts[0])
    for cut in cuts[1:]:
        loudness = loudness * one(*cut)
    return loudness


def centred(own_key, shape, scale, limit, shards=(), held_as=jnp.bfloat16):
    loudness = shard_levels(own_key, shape, shards, -0.22, 0.18) if shards else 1.0
    values = jax.random.normal(own_key, shape, jnp.float32) * scale * loudness
    return jnp.minimum(jnp.maximum(values, -limit), limit).astype(held_as)


def noise_with(stream_key, dims, width, limit, cuts, heavy, kind=jnp.bfloat16):
    values = width * jax.random.normal(stream_key, dims, jnp.float32)
    if cuts:
        values = values * shard_levels(stream_key, dims, cuts, -0.22, 0.18)
    return jnp.clip(strengthened(values, jax.random.fold_in(stream_key, 3), *heavy), -limit, limit).astype(kind)


def setup_inputs(seed: int = 0, part: int = 0) -> dict:
    seeds = jax.random.split(jax.random.key(seed), 7)
    part_splits = jax.random.split(jax.random.fold_in(seeds[6], part), 7)
    return {
        "head_inputs": centred(part_splits[0], (3, SCAN_SAMPLES, PIECE_ELEMENTS, ATTENTION_SPLITS * P_SIZE), 0.05, 0.29882812, ((1, 2), (2, 4), (3, 2))),
        "write_read": centred(part_splits[1], (3, SCAN_SAMPLES, PIECE_ELEMENTS, 2 * N), 0.045, 0.26953125, ((1, 2), (2, 4))),
        "decay_steps": draw_decay_steps(jax.random.fold_in(jax.random.fold_in(seeds[6], part), 71), part),
        "scan_orders": draw_scan_orders(jax.random.fold_in(jax.random.fold_in(seeds[6], part), 71), part),
        "cotangent": noise_with(part_splits[4], (SCAN_SAMPLES, PIECE_ELEMENTS, D), 0.1, 0.59765625, ((0, 2), (1, 4)), (1, 2, 4, 2.0)),
        "out_weight": centred(seeds[5], (3, D, ATTENTION_SPLITS * P_SIZE), (ATTENTION_SPLITS * P_SIZE // 8) ** -0.5, 0.4375, ((1, 4), (2, 2))),
    }


EXACT = lax.Precision.HIGHEST


def contract(form, *operands):
    return jnp.einsum(form, *operands, precision=EXACT)


def segment_parts(log_rates, writes, readers):
    running = jnp.cumsum(log_rates, axis=-1)
    final_log = running[..., -1]
    length = log_rates.shape[-1]
    causal = jnp.arange(length)[:, None] >= jnp.arange(length)[None, :]
    differ = jnp.where(causal, running[..., :, None] - running[..., None, :], 0.0)
    decay_mat = jnp.where(causal, jnp.exp(differ), 0.0)
    scores = contract("ovin,ovjn->ovij", readers, writes)
    mixing = scores[:, :, None] * decay_mat
    return running, final_log, decay_mat, mixing


def segment_forward(pieces, signal, writes, readers, memory):
    running, final_log, decay_mat, mixing = pieces
    rising = jnp.exp(running)
    falling = jnp.exp(final_log[..., None] - running)
    outputs = contract("ovhij,ovjhp->ovihp", mixing, signal) + contract("ovhi,ovin,ovhnp->ovihp", rising, readers, memory)
    memory_next = jnp.exp(final_log)[..., None, None] * memory + contract("ovhj,ovjn,ovjhp->ovhnp", falling, writes, signal)
    return outputs, memory_next


def segment_backward(pieces, signal, writes, readers, upstream, memory, memory_grad):
    running, final_log, decay_mat, mixing = pieces
    rising = jnp.exp(running)
    falling = jnp.exp(final_log[..., None] - running)
    grad_signal = contract("ovhij,ovihp->ovjhp", mixing, upstream) + contract("ovhj,ovjn,ovhnp->ovjhp", falling, writes, memory_grad)
    weighted = contract("ovihp,ovjhp->ovhij", upstream, signal) * decay_mat
    grad_writes = contract("ovhij,ovin->ovjn", weighted, readers) + contract("ovhj,ovjhp,ovhnp->ovjn", falling, signal, memory_grad)
    grad_readers = contract("ovhij,ovjn->ovin", weighted, writes) + contract("ovhi,ovihp,ovhnp->ovin", rising, upstream, memory)
    grad_prev = jnp.exp(final_log)[..., None, None] * memory_grad + contract("ovhi,ovin,ovihp->ovhnp", rising, readers, upstream)
    return grad_signal, grad_writes, grad_readers, grad_prev


def run_segments(signal, writes, readers, log_rates, upstream, memory_in, grad_in, length):
    blocks = signal.shape[2] // length

    def cut_rows(array, number, along):
        start_row = (number * length).astype(jnp.int32)
        return lax.dynamic_slice_in_dim(array, start_row, length, along)

    def forward_turn(number, carried):
        memory, outputs, memories = carried
        sig = cut_rows(signal, number, 2)
        wri = cut_rows(writes, number, 2)
        rea = cut_rows(readers, number, 2)
        pieces = segment_parts(cut_rows(log_rates, number, 3), wri, rea)
        out_rows, memory_next = segment_forward(pieces, sig, wri, rea, memory)
        outputs = lax.dynamic_update_slice_in_dim(outputs, out_rows, (number * length).astype(jnp.int32), 2)
        memories = lax.dynamic_update_index_in_dim(memories, memory, number, 0)
        return memory_next, outputs, memories

    start_memories = jnp.zeros((blocks,) + memory_in.shape, memory_in.dtype)
    _, outputs, memories = lax.fori_loop(0, blocks, forward_turn, (memory_in, jnp.zeros_like(signal), start_memories))

    def backward_turn(countdown, carried):
        memory_grad, grad_signal, grad_writes, grad_readers = carried
        number = blocks - 1 - countdown
        sig = cut_rows(signal, number, 2)
        wri = cut_rows(writes, number, 2)
        rea = cut_rows(readers, number, 2)
        pieces = segment_parts(cut_rows(log_rates, number, 3), wri, rea)
        memory = lax.dynamic_index_in_dim(memories, number, 0, keepdims=False)
        part_sig, part_wri, part_rea, grad_prev = segment_backward(pieces, sig, wri, rea, cut_rows(upstream, number, 2), memory, memory_grad)
        start_row = (number * length).astype(jnp.int32)
        grad_signal = lax.dynamic_update_slice_in_dim(grad_signal, part_sig, start_row, 2)
        grad_writes = lax.dynamic_update_slice_in_dim(grad_writes, part_wri, start_row, 2)
        grad_readers = lax.dynamic_update_slice_in_dim(grad_readers, part_rea, start_row, 2)
        return grad_prev, grad_signal, grad_writes, grad_readers

    _, grad_signal, grad_writes, grad_readers = lax.fori_loop(0, blocks, backward_turn, (grad_in, jnp.zeros_like(signal), jnp.zeros_like(writes), jnp.zeros_like(readers)))
    return outputs, grad_signal, grad_writes, grad_readers


def reference(head_inputs, write_read, decay_steps, scan_orders, cotangent, out_weight):
    inner_width = ATTENTION_SPLITS * P_SIZE
    length = math.gcd(PIECE_ELEMENTS, 128)
    grads_inputs = []
    grads_wr = []
    grads_weight = []
    for orient in range(3):
        if orient == 0:
            scanned = cotangent
        else:
            scanned = jax.vmap(lambda table_rows, row_ids: table_rows[row_ids])(cotangent, scan_orders[orient - 1])
        flat_rows = scanned.reshape(SCAN_SAMPLES * PIECE_ELEMENTS, D)
        upstream = jnp.dot(flat_rows, out_weight[orient], preferred_element_type=jnp.float32).astype(jnp.bfloat16)
        upstream = lax.optimization_barrier(upstream)
        signal = head_inputs[orient].astype(jnp.float32).reshape(1, SCAN_SAMPLES, PIECE_ELEMENTS, ATTENTION_SPLITS, P_SIZE)
        writes = write_read[orient, :, :, :N].astype(jnp.float32)[None]
        readers = write_read[orient, :, :, N:].astype(jnp.float32)[None]
        log_rates = (-decay_steps[orient].astype(jnp.float32) / PIECE_ELEMENTS)[None]
        grad_up = upstream.astype(jnp.float32).reshape(1, SCAN_SAMPLES, PIECE_ELEMENTS, ATTENTION_SPLITS, P_SIZE)
        zero_memory = jnp.zeros((1, SCAN_SAMPLES, ATTENTION_SPLITS, N, P_SIZE), jnp.float32)
        outputs, grad_signal, grad_writes, grad_readers = run_segments(signal, writes, readers, log_rates, grad_up, zero_memory, zero_memory, length)
        outputs_bf = outputs.reshape(SCAN_SAMPLES * PIECE_ELEMENTS, inner_width).astype(jnp.bfloat16)
        grads_weight.append(jnp.dot(flat_rows.T, outputs_bf, preferred_element_type=jnp.float32).astype(jnp.bfloat16))
        grads_inputs.append(grad_signal.reshape(SCAN_SAMPLES, PIECE_ELEMENTS, inner_width).astype(jnp.bfloat16))
        grads_wr.append(jnp.concatenate([grad_writes, grad_readers], axis=-1)[0].astype(jnp.bfloat16))
    return jnp.stack(grads_inputs), jnp.stack(grads_wr), jnp.stack(grads_weight)
```

```python
import functools
import math

import jax
import jax.numpy as jnp
from jax import lax
from jax.experimental import pallas as pl
from jax.experimental.pallas import tpu as pltpu
from jax.sharding import PartitionSpec as P

P_SIZE = 128
N = 64
F32 = jnp.float32
BF = jnp.bfloat16
MESH = pl.DeviceIdType.MESH


def dot(a, b, ca, cb):
    return lax.dot_general(a, b, (((ca,), (cb,)), ((), ())), preferred_element_type=F32)


def kernel(
    sizes, x_ref, wr_ref, steps_ref, orders_ref, cot_ref, w_ref,
    gx_ref, gwr_ref, gw_ref,
    sums, sums_in, cotg, wg, ends, ends_in, state, grads, grads_in, gout, scanned, mixing, outs, dys,
    pf, pb, pa_in, sb, sb_in, cb, cb_in, runc, runr, part, part_in,
    s_sum, r_sum, s_cot, r_cot, s_w, r_w, s_g, r_g, s_end, r_end, s_gr, r_gr, s_a, r_a, s_b, r_b,
    s_c, r_c, s_m, r_m,
):
    n, n_dp, n_gr, n_mp = sizes
    me = lax.axis_index("ctx")
    my_dp = lax.axis_index("dp")
    my_gr = lax.axis_index("groups")
    my_mp = lax.axis_index("mp")
    tokens, width = cot_ref.shape
    inner = x_ref.shape[2]
    heads = inner // P_SIZE
    rows = w_ref.shape[1]
    blk = tokens // n
    seq = tokens * n
    scale = -1.0 / seq
    wcol = inner // n_gr
    parts = math.gcd(inner // 128, n_dp)
    pcol = inner // parts

    def ctx_at(k):
        return lax.rem(me + k, n)

    def gr_at(k):
        return lax.rem(my_gr + k, n_gr)

    def dp_at(k):
        return lax.rem(my_dp + k, n_dp)

    my_part = lax.rem(my_dp, parts)
    base_dp = my_dp - my_part

    def pair_at(k):
        return base_dp + lax.rem(my_part + k, parts)

    def send(src, dst, ss, rs, where):
        return pltpu.make_async_remote_copy(
            src_ref=src, dst_ref=dst, send_sem=ss, recv_sem=rs, device_id=where, device_id_type=MESH
        )

    barrier = pltpu.get_barrier_semaphore()
    for k in range(1, n):
        pl.semaphore_signal(barrier, inc=1, device_id={"ctx": ctx_at(k)}, device_id_type=MESH)
    for k in range(1, n_gr):
        pl.semaphore_signal(barrier, inc=1, device_id={"groups": gr_at(k)}, device_id_type=MESH)
    for k in range(1, n_dp):
        pl.semaphore_signal(barrier, inc=1, device_id={"dp": dp_at(k)}, device_id_type=MESH)
    for k in range(1, n_mp):
        pl.semaphore_signal(barrier, inc=1, device_id={"mp": lax.rem(my_mp + k, n_mp)}, device_id_type=MESH)
    pl.semaphore_wait(barrier, n + n_gr + n_dp + n_mp - 4)

    def cot_copy(k):
        return send(
            cot_ref.at[pl.ds(pl.multiple_of(ctx_at(k) * blk, blk), blk)],
            cotg.at[pl.ds(pl.multiple_of(me * blk, blk), blk)],
            s_cot.at[k], r_cot.at[k], {"ctx": ctx_at(k)},
        )

    def w_copy(k):
        cols = pl.ds(pl.multiple_of(my_gr * wcol, 128), wcol)
        return send(
            w_ref.at[:, :, cols],
            wg.at[:, pl.ds(pl.multiple_of(me * rows, rows), rows), cols],
            s_w.at[k], r_w.at[k], {"ctx": ctx_at(k)},
        )

    def g_copy(k, g):
        owner = lax.rem(me + n - k, n)
        piece = wg.at[
            :, pl.ds(pl.multiple_of(owner * rows, rows), rows), pl.ds(pl.multiple_of(my_gr * wcol, 128), wcol)
        ]
        return send(piece, piece, s_g.at[k, g], r_g.at[k, g], {"groups": gr_at(g)})

    def sum_copy(k):
        return send(sums, sums_in.at[k], s_sum.at[k], r_sum.at[k], {"ctx": ctx_at(k)})

    for k in range(1, n):
        cot_copy(k).start()
    lower = (
        lax.broadcasted_iota(jnp.int32, (tokens, tokens), 0)
        >= lax.broadcasted_iota(jnp.int32, (tokens, tokens), 1)
    )
    tri = jnp.where(lower, 1.0, 0.0).astype(BF)

    def running(o, _):
        steps = steps_ref[o]
        high = (steps // 256).astype(F32).astype(BF)
        low = (steps % 256).astype(F32).astype(BF)
        runr[o] = dot(high, tri, 1, 1) * 256.0 + dot(low, tri, 1, 1)
        runc[o] = dot(tri, high, 1, 1) * 256.0 + dot(tri, low, 1, 1)
        sums[o] = jnp.broadcast_to(runr[o][:, tokens - 1 :] * scale, sums.shape[1:])
        return 0

    lax.fori_loop(0, 3, running, 0)
    for k in range(1, n):
        sum_copy(k).start()
    for k in range(1, n):
        w_copy(k).start()

    def end_states(o, _):
        bt = wr_ref[o][:, :N]
        rc = runc[o] * scale
        falling = jnp.exp(rc[tokens - 1 :, :] - rc)
        for h in range(heads):
            xs = (x_ref[o, :, h * P_SIZE : (h + 1) * P_SIZE].astype(F32) * falling[:, h : h + 1]).astype(BF)
            ends[o, h] = dot(bt, xs, 0, 0).astype(BF)
        return 0

    lax.fori_loop(0, 3, end_states, 0)

    def end_copy(k):
        return send(ends, ends_in.at[k], s_end.at[k], r_end.at[k], {"ctx": ctx_at(k)})

    def grad_copy(k):
        return send(grads, grads_in.at[k], s_gr.at[k], r_gr.at[k], {"ctx": lax.rem(me + n - k, n)})

    for k in range(1, n):

        @pl.when(me + k < n)
        def _():
            end_copy(k).start()

    cotg[pl.ds(pl.multiple_of(me * blk, blk), blk), :] = cot_ref[pl.ds(pl.multiple_of(me * blk, blk), blk), :]
    wg[:, pl.ds(pl.multiple_of(me * rows, rows), rows), :] = w_ref[...]
    for k in range(1, n):
        cot_copy(k).wait()
    scanned[0] = cot_ref[...]

    def permute(o, _):
        ids = orders_ref[o]
        place = (ids // tokens) * blk + ids % blk
        hot = jnp.where(lax.broadcasted_iota(jnp.int32, (tokens, tokens), 0) == place, 1.0, 0.0).astype(BF)
        scanned[o + 1] = dot(hot, cotg[...], 0, 0).astype(BF)
        return 0

    lax.fori_loop(0, 2, permute, 0)

    state[...] = jnp.zeros_like(state)
    gout[...] = jnp.zeros_like(gout)
    for k in range(1, n):
        sum_copy(k).wait()

    def gather_states(total, got, copy_of, mine, sums_at):
        for k in range(1, n):

            @pl.when(mine >= k)
            def _():
                copy_of(k).wait_recv()

                def one(o, _):
                    log = jnp.zeros(sums.shape[1:], F32)
                    for j in range(1, k):
                        log = log + sums_in[sums_at(j), o]
                    fade = jnp.exp(log)
                    for h in range(heads):
                        total[o, h] = total[o, h] + fade[h : h + 1, :] * got[k, o, h].astype(F32)
                    return 0

                lax.fori_loop(0, 3, one, 0)

    gather_states(state, ends_in, end_copy, me, lambda j: j)

    def pair_copy(k, o):
        cols = pl.ds(pl.multiple_of((pair_at(k) - base_dp) * pcol, 128), pcol)
        return send(
            pb.at[o, :, cols], pa_in.at[k, o], s_a.at[k, o], r_a.at[k, o], {"dp": pair_at(k)}
        )

    def forward(o, _):
        bt = wr_ref[o][:, :N]
        ct = wr_ref[o][:, N:]
        scores = dot(ct, bt, 1, 1)
        rc = runc[o] * scale
        rr = runr[o] * scale
        rising = jnp.exp(rc)
        for h in range(heads):
            cut = slice(h * P_SIZE, (h + 1) * P_SIZE)
            decay = jnp.where(lower, jnp.exp(jnp.minimum(rc[:, h : h + 1] - rr[h : h + 1, :], 0.0)), 0.0)
            mix = (scores * decay).astype(BF)
            mixing[o, h] = mix
            up = (ct.astype(F32) * rising[:, h : h + 1]).astype(BF)
            outs[:, cut] = (
                dot(mix, x_ref[o, :, cut], 1, 0) + dot(up, state[o, h].astype(BF), 1, 0)
            ).astype(BF)
        term = dot(scanned[o], outs[...], 0, 0)
        pf[o] = term
        pb[o] = term.astype(BF)
        for k in range(1, parts):
            pair_copy(k, o).start()
        return 0

    lax.fori_loop(0, 3, forward, 0)

    for k in range(1, n):
        w_copy(k).wait()
        for g in range(1, n_gr):
            g_copy(k, g).start()
    for k in range(1, n):
        for g in range(1, n_gr):
            g_copy(k, g).wait()

    def upstream(o, _):
        ct = wr_ref[o][:, N:]
        dys[o] = dot(scanned[o], wg[o], 1, 0).astype(BF)
        rising = jnp.exp(runc[o] * scale)
        for h in range(heads):
            up = (ct.astype(F32) * rising[:, h : h + 1]).astype(BF)
            grads[o, h] = dot(up, dys[o, :, h * P_SIZE : (h + 1) * P_SIZE], 0, 0).astype(BF)
        return 0

    lax.fori_loop(0, 3, upstream, 0)
    for k in range(1, n):

        @pl.when(me >= k)
        def _():
            grad_copy(k).start()

    mine_cols = pl.ds(pl.multiple_of(my_part * pcol, 128), pcol)

    def ctx_copy(k, o):
        return send(
            sb.at[o, pl.ds(pl.multiple_of(ctx_at(k) * rows, rows), rows)],
            sb_in.at[k, o], s_b.at[k, o], r_b.at[k, o], {"ctx": ctx_at(k)},
        )

    def pair_sum(o, _):
        total = pf[o, :, mine_cols]
        for k in range(1, parts):
            pair_copy(k, o).wait()
            total = total + pa_in[k, o].astype(F32)
        pf[o, :, mine_cols] = total
        sb[o] = total.astype(BF)
        for k in range(1, n):
            ctx_copy(k, o).start()
        return 0

    lax.fori_loop(0, 3, pair_sum, 0)
    gather_states(gout, grads_in, grad_copy, n - 1 - me, lambda j: n - j)

    def backward(o, _):
        bt = wr_ref[o][:, :N]
        ct = wr_ref[o][:, N:]
        rc = runc[o] * scale
        rr = runr[o] * scale
        rising = jnp.exp(rc)
        falling = jnp.exp(rc[tokens - 1 :, :] - rc)
        both = jnp.zeros((tokens, tokens), F32)
        gb = jnp.zeros((tokens, N), F32)
        gc = jnp.zeros((tokens, N), F32)
        for h in range(heads):
            cut = slice(h * P_SIZE, (h + 1) * P_SIZE)
            xs = x_ref[o, :, cut]
            dy = dys[o, :, cut]
            far = gout[o, h].astype(BF)
            down = (bt.astype(F32) * falling[:, h : h + 1]).astype(BF)
            gx_ref[o, :, cut] = (dot(mixing[o, h], dy, 0, 0) + dot(down, far, 1, 0)).astype(BF)
            decay = jnp.where(lower, jnp.exp(jnp.minimum(rc[:, h : h + 1] - rr[h : h + 1, :], 0.0)), 0.0)
            both = both + dot(dy, xs, 1, 1) * decay
            gb = gb + falling[:, h : h + 1] * dot(xs, far, 1, 1)
            gc = gc + rising[:, h : h + 1] * dot(dy, state[o, h].astype(BF), 1, 1)
        both = both.astype(BF)
        part[o, :, :N] = gb + dot(both, ct, 0, 0)
        part[o, :, N:] = gc + dot(both, bt, 1, 0)
        return 0

    lax.fori_loop(0, 3, backward, 0)

    def mp_copy(k):
        return send(part, part_in.at[k], s_m.at[k], r_m.at[k], {"mp": lax.rem(my_mp + k, n_mp)})

    for k in range(1, n_mp):
        mp_copy(k).start()

    def dp_copy(k):
        return send(cb, cb_in.at[k], s_c.at[k], r_c.at[k], {"dp": dp_at(k)})

    def ctx_sum(o, _):
        total = pf[o, pl.ds(pl.multiple_of(me * rows, rows), rows), mine_cols]
        for k in range(1, n):
            ctx_copy(k, o).wait()
            total = total + sb_in[k, o].astype(F32)
        cb[o] = total.astype(BF)
        return 0

    lax.fori_loop(0, 3, ctx_sum, 0)
    for k in range(1, n_dp):
        dp_copy(k).start()
    for k in range(1, n_mp):
        mp_copy(k).wait()
    total = part[...]
    for k in range(1, n_mp):
        total = total + part_in[k]
    gwr_ref[...] = total.astype(BF)
    for k in range(1, n_dp):
        dp_copy(k).wait()
    for u in range(parts):
        sum_u = jnp.zeros((3, rows, pcol), F32)
        own = cb[...].astype(F32)
        for k in range(n_dp):
            piece = own if k == 0 else cb_in[k].astype(F32)
            belongs = lax.rem(my_dp + n_dp - k, parts) == u
            sum_u = sum_u + jnp.where(belongs, piece, 0.0)
        gw_ref[:, :, u * pcol : (u + 1) * pcol] = sum_u.astype(BF)

    for k in range(1, n):

        @pl.when(me + k < n)
        def _():
            end_copy(k).wait_send()

        @pl.when(me >= k)
        def _():
            grad_copy(k).wait_send()


def shards(sizes, head_inputs, write_read, decay_steps, scan_orders, cotangent, out_weight):
    n, n_dp, n_gr, n_mp = sizes
    tokens, width = cotangent.shape[1:]
    inner = head_inputs.shape[3]
    heads = decay_steps.shape[2]
    rows = out_weight.shape[1]
    parts = math.gcd(inner // 128, n_dp)
    pcol = inner // parts
    x = head_inputs.reshape(3, tokens, inner)
    wr = write_read.reshape(3, tokens, 2 * N)
    steps = jnp.pad(decay_steps.reshape(3, heads, tokens), ((0, 0), (0, -heads % 8), (0, 0)))
    hp = steps.shape[1]
    V = pltpu.VMEM
    dma = pltpu.SemaphoreType.DMA
    scratch = [
        V((3, hp, 128), F32), V((n, 3, hp, 128), F32), V((tokens, width), BF), V((3, width, inner), BF),
        V((3, heads, N, P_SIZE), BF), V((n, 3, heads, N, P_SIZE), BF), V((3, heads, N, P_SIZE), F32),
        V((3, heads, N, P_SIZE), BF), V((n, 3, heads, N, P_SIZE), BF), V((3, heads, N, P_SIZE), F32),
        V((3, tokens, width), BF), V((3, heads, tokens, tokens), BF), V((tokens, inner), BF),
        V((3, tokens, inner), BF),
        V((3, width, inner), F32), V((3, width, inner), BF), V((parts, 3, width, pcol), BF),
        V((3, width, pcol), BF), V((n, 3, rows, pcol), BF), V((3, rows, pcol), BF), V((n_dp, 3, rows, pcol), BF),
        V((3, tokens, hp), F32), V((3, hp, tokens), F32),
        V((3, tokens, 2 * N), F32), V((n_mp, 3, tokens, 2 * N), F32),
        dma((n,)), dma((n,)), dma((n,)), dma((n,)), dma((n,)), dma((n,)), dma((n, n_gr)), dma((n, n_gr)),
        dma((n,)), dma((n,)), dma((n,)), dma((n,)), dma((parts, 3)), dma((parts, 3)), dma((n, 3)), dma((n, 3)),
        dma((n_dp,)), dma((n_dp,)), dma((n_mp,)), dma((n_mp,)),
    ]
    gx, gwr, gw = pl.pallas_call(
        functools.partial(kernel, sizes),
        out_shape=(
            jax.ShapeDtypeStruct((3, tokens, inner), BF),
            jax.ShapeDtypeStruct((3, tokens, 2 * N), BF),
            jax.ShapeDtypeStruct((3, rows, inner), BF),
        ),
        in_specs=[pl.BlockSpec(memory_space=V)] * 6,
        out_specs=(pl.BlockSpec(memory_space=V),) * 3,
        scratch_shapes=scratch,
        compiler_params=pltpu.CompilerParams(
            collective_id=0, has_side_effects=True, vmem_limit_bytes=60 * 2**20
        ),
    )(x, wr, steps, scan_orders.reshape(2, 1, tokens), cotangent.reshape(tokens, width), out_weight)
    return gx[:, None], gwr[:, None], gw


def solution(mesh):
    sizes = (mesh.shape["ctx"], mesh.shape["dp"], mesh.shape["groups"], mesh.shape["mp"])
    in_specs = (
        P(None, ("groups", "dp"), "ctx", "mp"),
        P(None, ("groups", "dp"), "ctx", None),
        P(None, ("groups", "dp"), "mp", "ctx"),
        P(None, ("groups", "dp"), "ctx"),
        P(("groups", "dp"), "ctx", None),
        P(None, "ctx", "mp"),
    )
    out_specs = (
        P(None, ("groups", "dp"), "ctx", "mp"),
        P(None, ("groups", "dp"), "ctx", None),
        P("groups", "ctx", "mp"),
    )
    return jax.shard_map(
        functools.partial(shards, sizes), mesh=mesh, in_specs=in_specs, out_specs=out_specs, check_vma=False
    )
```

```python
import functools
import math

import jax
import jax.numpy as jnp
from jax import lax
from jax.experimental import pallas as pl
from jax.experimental.pallas import tpu as pltpu
from jax.sharding import PartitionSpec as P

P_SIZE = 128
N = 64
F32 = jnp.float32
BF = jnp.bfloat16
MESH = pl.DeviceIdType.MESH


def dot(a, b, ca, cb):
    return lax.dot_general(a, b, (((ca,), (cb,)), ((), ())), preferred_element_type=F32)


def kernel(
    sizes, x_ref, wr_ref, steps_ref, orders_ref, cot_ref, w_ref,
    gx_ref, gwr_ref, gw_ref,
    cotg, wg, ends, ends_out, ends_in, state, grads, grads_out, grads_in, gout, scanned, mixing, outs, dys,
    pf, pb, pa_in, sb, sb_in, cb, cb_in, runc, runr, part, part_in,
    s_cot, r_cot, s_w, r_w, s_g, r_g, s_end, r_end, s_gr, r_gr, s_a, r_a, s_b, r_b,
    s_c, r_c, s_m, r_m,
):
    n, n_dp, n_gr, n_mp = sizes
    me = lax.axis_index("ctx")
    my_dp = lax.axis_index("dp")
    my_gr = lax.axis_index("groups")
    my_mp = lax.axis_index("mp")
    tokens, width = cot_ref.shape
    inner = x_ref.shape[2]
    heads = inner // P_SIZE
    rows = w_ref.shape[1]
    blk = tokens // n
    seq = tokens * n
    scale = -1.0 / seq
    wcol = inner // n_gr
    parts = math.gcd(inner // 128, n_dp)
    pcol = inner // parts

    def ctx_at(k):
        return lax.rem(me + k, n)

    def gr_at(k):
        return lax.rem(my_gr + k, n_gr)

    def dp_at(k):
        return lax.rem(my_dp + k, n_dp)

    my_part = lax.rem(my_dp, parts)
    base_dp = my_dp - my_part

    def pair_at(k):
        return base_dp + lax.rem(my_part + k, parts)

    def send(src, dst, ss, rs, where):
        return pltpu.make_async_remote_copy(
            src_ref=src, dst_ref=dst, send_sem=ss, recv_sem=rs, device_id=where, device_id_type=MESH
        )

    barrier = pltpu.get_barrier_semaphore()
    for k in range(1, n):
        pl.semaphore_signal(barrier, inc=1, device_id={"ctx": ctx_at(k)}, device_id_type=MESH)
    for k in range(1, n_gr):
        pl.semaphore_signal(barrier, inc=1, device_id={"groups": gr_at(k)}, device_id_type=MESH)
    for k in range(1, n_dp):
        pl.semaphore_signal(barrier, inc=1, device_id={"dp": dp_at(k)}, device_id_type=MESH)
    for k in range(1, n_mp):
        pl.semaphore_signal(barrier, inc=1, device_id={"mp": lax.rem(my_mp + k, n_mp)}, device_id_type=MESH)
    pl.semaphore_wait(barrier, n + n_gr + n_dp + n_mp - 4)

    def cot_copy(k):
        return send(
            cot_ref.at[pl.ds(pl.multiple_of(ctx_at(k) * blk, blk), blk)],
            cotg.at[pl.ds(pl.multiple_of(me * blk, blk), blk)],
            s_cot.at[k], r_cot.at[k], {"ctx": ctx_at(k)},
        )

    def w_copy(k):
        cols = pl.ds(pl.multiple_of(my_gr * wcol, 128), wcol)
        return send(
            w_ref.at[:, :, cols],
            wg.at[:, pl.ds(pl.multiple_of(me * rows, rows), rows), cols],
            s_w.at[k], r_w.at[k], {"ctx": ctx_at(k)},
        )

    def g_copy(k, g):
        owner = lax.rem(me + n - k, n)
        piece = wg.at[
            :, pl.ds(pl.multiple_of(owner * rows, rows), rows), pl.ds(pl.multiple_of(my_gr * wcol, 128), wcol)
        ]
        return send(piece, piece, s_g.at[k, g], r_g.at[k, g], {"groups": gr_at(g)})

    for k in range(1, n):
        cot_copy(k).start()
    for k in range(1, n):
        w_copy(k).start()
    lower = (
        lax.broadcasted_iota(jnp.int32, (tokens, tokens), 0)
        >= lax.broadcasted_iota(jnp.int32, (tokens, tokens), 1)
    )
    tri = jnp.where(lower, 1.0, 0.0).astype(BF)

    def running(o, _):
        steps = steps_ref[o]
        high = (steps // 256).astype(F32).astype(BF)
        low = (steps % 256).astype(F32).astype(BF)
        runr[o] = dot(high, tri, 1, 1) * 256.0 + dot(low, tri, 1, 1)
        runc[o] = dot(tri, high, 1, 1) * 256.0 + dot(tri, low, 1, 1)
        return 0

    lax.fori_loop(0, 3, running, 0)

    def end_states(o, _):
        bt = wr_ref[o][:, :N]
        rc = runc[o] * scale
        falling = jnp.exp(rc[tokens - 1 :, :] - rc)
        for h in range(heads):
            xs = (x_ref[o, :, h * P_SIZE : (h + 1) * P_SIZE].astype(F32) * falling[:, h : h + 1]).astype(BF)
            ends[o, h] = dot(bt, xs, 0, 0)
        return 0

    lax.fori_loop(0, 3, end_states, 0)

    def end_copy(o):
        return send(ends_out.at[o], ends_in.at[o], s_end.at[o], r_end.at[o], {"ctx": lax.rem(me + 1, n)})

    def grad_copy(o):
        return send(grads_out.at[o], grads_in.at[o], s_gr.at[o], r_gr.at[o], {"ctx": lax.rem(me + n - 1, n)})

    def chain(o, copy_of, total, own, outgoing, incoming, first, last):
        @pl.when(jnp.logical_not(first))
        def _():
            copy_of(o).wait_recv()
            total[o] = incoming[o].astype(F32)

        @pl.when(jnp.logical_not(last))
        def _():
            fade = jnp.exp(runr[o][:, tokens - 1 :] * scale)
            for h in range(heads):
                outgoing[o, h] = (total[o, h] * fade[h : h + 1, :] + own[o, h]).astype(outgoing.dtype)
            copy_of(o).start()

    cotg[pl.ds(pl.multiple_of(me * blk, blk), blk), :] = cot_ref[pl.ds(pl.multiple_of(me * blk, blk), blk), :]
    wg[:, pl.ds(pl.multiple_of(me * rows, rows), rows), :] = w_ref[...]
    for k in range(1, n):
        cot_copy(k).wait()
    scanned[0] = cot_ref[...]

    def permute(o, _):
        ids = orders_ref[o]
        place = (ids // tokens) * blk + ids % blk
        hot = jnp.where(lax.broadcasted_iota(jnp.int32, (tokens, tokens), 0) == place, 1.0, 0.0).astype(BF)
        scanned[o + 1] = dot(hot, cotg[...], 0, 0).astype(BF)
        return 0

    lax.fori_loop(0, 2, permute, 0)

    state[...] = jnp.zeros_like(state)
    gout[...] = jnp.zeros_like(gout)
    def pair_copy(k, o):
        cols = pl.ds(pl.multiple_of((pair_at(k) - base_dp) * pcol, 128), pcol)
        return send(
            pb.at[o, :, cols], pa_in.at[k, o], s_a.at[k, o], r_a.at[k, o], {"dp": pair_at(k)}
        )

    def forward(o, _):
        chain(o, end_copy, state, ends, ends_out, ends_in, me == 0, me == n - 1)
        bt = wr_ref[o][:, :N]
        ct = wr_ref[o][:, N:]
        scores = dot(ct, bt, 1, 1)
        rc = runc[o] * scale
        rr = runr[o] * scale
        rising = jnp.exp(rc)
        for h in range(heads):
            cut = slice(h * P_SIZE, (h + 1) * P_SIZE)
            decay = jnp.where(lower, jnp.exp(jnp.minimum(rc[:, h : h + 1] - rr[h : h + 1, :], 0.0)), 0.0)
            full = scores * decay
            mix = full.astype(BF)
            rest = (full - mix.astype(F32)).astype(BF)
            mixing[o, h] = mix
            up = (ct.astype(F32) * rising[:, h : h + 1]).astype(BF)
            outs[:, cut] = (
                dot(mix, x_ref[o, :, cut], 1, 0)
                + dot(rest, x_ref[o, :, cut], 1, 0)
                + dot(up, state[o, h].astype(BF), 1, 0)
            ).astype(BF)
        term = dot(scanned[o], outs[...], 0, 0)
        pf[o] = term
        pb[o] = term.astype(BF)
        for k in range(1, parts):
            pair_copy(k, o).start()
        return 0

    lax.fori_loop(0, 3, forward, 0)

    mine_cols = pl.ds(pl.multiple_of(my_part * pcol, 128), pcol)

    def ctx_copy(k, o):
        return send(
            sb.at[o, pl.ds(pl.multiple_of(ctx_at(k) * rows, rows), rows)],
            sb_in.at[k, o], s_b.at[k, o], r_b.at[k, o], {"ctx": ctx_at(k)},
        )

    def pair_sum(o, _):
        total = pf[o, :, mine_cols]
        for k in range(1, parts):
            pair_copy(k, o).wait()
            total = total + pa_in[k, o].astype(F32)
        pf[o, :, mine_cols] = total
        sb[o] = total.astype(BF)
        for k in range(1, n):
            ctx_copy(k, o).start()
        return 0

    for k in range(1, n):
        w_copy(k).wait()
        for g in range(1, n_gr):
            g_copy(k, g).start()
        if k == 1:
            pair_sum(0, 0)
    pair_sum(1, 0)
    for k in range(1, n):
        for g in range(1, n_gr):
            g_copy(k, g).wait()

    def upstream(o, _):
        ct = wr_ref[o][:, N:]
        dys[o] = dot(scanned[o], wg[o], 1, 0).astype(BF)
        rising = jnp.exp(runc[o] * scale)
        for h in range(heads):
            up = (ct.astype(F32) * rising[:, h : h + 1]).astype(BF)
            grads[o, h] = dot(up, dys[o, :, h * P_SIZE : (h + 1) * P_SIZE], 0, 0)
        return 0

    lax.fori_loop(0, 3, upstream, 0)
    pair_sum(2, 0)

    def dp_copy(k, o):
        return send(cb.at[o], cb_in.at[k, o], s_c.at[k, o], r_c.at[k, o], {"dp": dp_at(k)})

    def ctx_sum(o):
        total = pf[o, pl.ds(pl.multiple_of(me * rows, rows), rows), mine_cols]
        for k in range(1, n):
            ctx_copy(k, o).wait()
            total = total + sb_in[k, o].astype(F32)
        cb[o] = total.astype(BF)
        for k in range(1, n_dp):
            dp_copy(k, o).start()

    def backward(o, _):
        chain(o, grad_copy, gout, grads, grads_out, grads_in, me == n - 1, me == 0)
        bt = wr_ref[o][:, :N]
        ct = wr_ref[o][:, N:]
        rc = runc[o] * scale
        rr = runr[o] * scale
        rising = jnp.exp(rc)
        falling = jnp.exp(rc[tokens - 1 :, :] - rc)
        both = jnp.zeros((tokens, tokens), F32)
        gb = jnp.zeros((tokens, N), F32)
        gc = jnp.zeros((tokens, N), F32)
        for h in range(heads):
            cut = slice(h * P_SIZE, (h + 1) * P_SIZE)
            xs = x_ref[o, :, cut]
            dy = dys[o, :, cut]
            far = gout[o, h].astype(BF)
            down = (bt.astype(F32) * falling[:, h : h + 1]).astype(BF)
            gx_ref[o, :, cut] = (dot(mixing[o, h], dy, 0, 0) + dot(down, far, 1, 0)).astype(BF)
            decay = jnp.where(lower, jnp.exp(jnp.minimum(rc[:, h : h + 1] - rr[h : h + 1, :], 0.0)), 0.0)
            both = both + dot(dy, xs, 1, 1) * decay
            gb = gb + falling[:, h : h + 1] * dot(xs, far, 1, 1)
            gc = gc + rising[:, h : h + 1] * dot(dy, state[o, h].astype(BF), 1, 1)
        both = both.astype(BF)
        part[o, :, :N] = gb + dot(both, ct, 0, 0)
        part[o, :, N:] = gc + dot(both, bt, 1, 0)

        @pl.when(o < 2)
        def _():
            ctx_sum(o)

        return 0

    lax.fori_loop(0, 3, backward, 0)

    def mp_copy(k):
        return send(part, part_in.at[k], s_m.at[k], r_m.at[k], {"mp": lax.rem(my_mp + k, n_mp)})

    for k in range(1, n_mp):
        mp_copy(k).start()

    ctx_sum(2)
    for k in range(1, n_mp):
        mp_copy(k).wait()
    total = part[...]
    for k in range(1, n_mp):
        total = total + part_in[k]
    gwr_ref[...] = total.astype(BF)
    for k in range(1, n_dp):
        for o in range(3):
            dp_copy(k, o).wait()
    for u in range(parts):
        sum_u = jnp.zeros((3, rows, pcol), F32)
        own = cb[...].astype(F32)
        for k in range(n_dp):
            piece = own if k == 0 else cb_in[k].astype(F32)
            belongs = lax.rem(my_dp + n_dp - k, parts) == u
            sum_u = sum_u + jnp.where(belongs, piece, 0.0)
        gw_ref[:, :, u * pcol : (u + 1) * pcol] = sum_u.astype(BF)

    for o in range(3):

        @pl.when(me < n - 1)
        def _():
            end_copy(o).wait_send()

        @pl.when(me > 0)
        def _():
            grad_copy(o).wait_send()


def shards(sizes, head_inputs, write_read, decay_steps, scan_orders, cotangent, out_weight):
    n, n_dp, n_gr, n_mp = sizes
    tokens, width = cotangent.shape[1:]
    inner = head_inputs.shape[3]
    heads = decay_steps.shape[2]
    rows = out_weight.shape[1]
    parts = math.gcd(inner // 128, n_dp)
    pcol = inner // parts
    x = head_inputs.reshape(3, tokens, inner)
    wr = write_read.reshape(3, tokens, 2 * N)
    steps = jnp.pad(decay_steps.reshape(3, heads, tokens), ((0, 0), (0, -heads % 8), (0, 0)))
    hp = steps.shape[1]
    chained = BF if n <= 4 else F32
    V = pltpu.VMEM
    dma = pltpu.SemaphoreType.DMA
    scratch = [
        V((tokens, width), BF), V((3, width, inner), BF),
        *[V((3, heads, N, P_SIZE), kind) for kind in (F32, chained, chained, F32)] * 2,
        V((3, tokens, width), BF), V((3, heads, tokens, tokens), BF), V((tokens, inner), BF),
        V((3, tokens, inner), BF),
        V((3, width, inner), F32), V((3, width, inner), BF), V((parts, 3, width, pcol), BF),
        V((3, width, pcol), BF), V((n, 3, rows, pcol), BF), V((3, rows, pcol), BF), V((n_dp, 3, rows, pcol), BF),
        V((3, tokens, hp), F32), V((3, hp, tokens), F32),
        V((3, tokens, 2 * N), F32), V((n_mp, 3, tokens, 2 * N), F32),
        dma((n,)), dma((n,)), dma((n,)), dma((n,)), dma((n, n_gr)), dma((n, n_gr)),
        dma((3,)), dma((3,)), dma((3,)), dma((3,)), dma((parts, 3)), dma((parts, 3)), dma((n, 3)), dma((n, 3)),
        dma((n_dp, 3)), dma((n_dp, 3)), dma((n_mp,)), dma((n_mp,)),
    ]
    gx, gwr, gw = pl.pallas_call(
        functools.partial(kernel, sizes),
        out_shape=(
            jax.ShapeDtypeStruct((3, tokens, inner), BF),
            jax.ShapeDtypeStruct((3, tokens, 2 * N), BF),
            jax.ShapeDtypeStruct((3, rows, inner), BF),
        ),
        in_specs=[pl.BlockSpec(memory_space=V)] * 6,
        out_specs=(pl.BlockSpec(memory_space=V),) * 3,
        scratch_shapes=scratch,
        compiler_params=pltpu.CompilerParams(
            collective_id=0, has_side_effects=True, vmem_limit_bytes=60 * 2**20
        ),
    )(x, wr, steps, scan_orders.reshape(2, 1, tokens), cotangent.reshape(tokens, width), out_weight)
    return gx[:, None], gwr[:, None], gw


def solution(mesh):
    sizes = (mesh.shape["ctx"], mesh.shape["dp"], mesh.shape["groups"], mesh.shape["mp"])
    in_specs = (
        P(None, ("groups", "dp"), "ctx", "mp"),
        P(None, ("groups", "dp"), "ctx", None),
        P(None, ("groups", "dp"), "mp", "ctx"),
        P(None, ("groups", "dp"), "ctx"),
        P(("groups", "dp"), "ctx", None),
        P(None, "ctx", "mp"),
    )
    out_specs = (
        P(None, ("groups", "dp"), "ctx", "mp"),
        P(None, ("groups", "dp"), "ctx", None),
        P("groups", "ctx", "mp"),
    )
    return jax.shard_map(
        functools.partial(shards, sizes), mesh=mesh, in_specs=in_specs, out_specs=out_specs, check_vma=False
    )
```

```python
import functools
import math

import jax
import jax.numpy as jnp
from jax import lax
from jax.experimental import pallas as pl
from jax.experimental.pallas import tpu as pltpu
from jax.sharding import PartitionSpec as P

P_SIZE = 128
N = 64
F32 = jnp.float32
BF = jnp.bfloat16
MESH = pl.DeviceIdType.MESH


def dot(a, b, ca, cb):
    return lax.dot_general(a, b, (((ca,), (cb,)), ((), ())), preferred_element_type=F32)


def kernel(
    sizes, x_ref, wr_ref, steps_ref, orders_ref, cot_ref, w_ref,
    gx_ref, gwr_ref, gw_ref,
    cotg, wg, ends, ends_out, ends_in, state, grads, grads_out, grads_in, gout, scanned, mixing, outs, dys,
    pf, pb, pa_in, sb, sb_in, cb, cb_in, runc, runr, part, part_in,
    s_cot, r_cot, s_w, r_w, s_g, r_g, s_end, r_end, s_gr, r_gr, s_a, r_a, s_b, r_b,
    s_c, r_c, s_m, r_m,
):
    n, n_dp, n_gr, n_mp = sizes
    me = lax.axis_index("ctx")
    my_dp = lax.axis_index("dp")
    my_gr = lax.axis_index("groups")
    my_mp = lax.axis_index("mp")
    tokens, width = cot_ref.shape
    inner = x_ref.shape[2]
    heads = inner // P_SIZE
    rows = w_ref.shape[1]
    blk = tokens // n
    seq = tokens * n
    scale = -1.0 / seq
    wcol = inner // n_gr
    parts = math.gcd(inner // 128, n_dp)
    pcol = inner // parts

    def ctx_at(k):
        return lax.rem(me + k, n)

    def gr_at(k):
        return lax.rem(my_gr + k, n_gr)

    def dp_at(k):
        return lax.rem(my_dp + k, n_dp)

    my_part = lax.rem(my_dp, parts)
    base_dp = my_dp - my_part

    def pair_at(k):
        return base_dp + lax.rem(my_part + k, parts)

    def send(src, dst, ss, rs, where):
        return pltpu.make_async_remote_copy(
            src_ref=src, dst_ref=dst, send_sem=ss, recv_sem=rs, device_id=where, device_id_type=MESH
        )

    barrier = pltpu.get_barrier_semaphore()
    for k in range(1, n):
        pl.semaphore_signal(barrier, inc=1, device_id={"ctx": ctx_at(k)}, device_id_type=MESH)
    for k in range(1, n_gr):
        pl.semaphore_signal(barrier, inc=1, device_id={"groups": gr_at(k)}, device_id_type=MESH)
    for k in range(1, n_dp):
        pl.semaphore_signal(barrier, inc=1, device_id={"dp": dp_at(k)}, device_id_type=MESH)
    for k in range(1, n_mp):
        pl.semaphore_signal(barrier, inc=1, device_id={"mp": lax.rem(my_mp + k, n_mp)}, device_id_type=MESH)
    pl.semaphore_wait(barrier, n + n_gr + n_dp + n_mp - 4)

    def cot_copy(k):
        return send(
            cot_ref.at[pl.ds(pl.multiple_of(ctx_at(k) * blk, blk), blk)],
            cotg.at[pl.ds(pl.multiple_of(me * blk, blk), blk)],
            s_cot.at[k], r_cot.at[k], {"ctx": ctx_at(k)},
        )

    def w_copy(k):
        cols = pl.ds(pl.multiple_of(my_gr * wcol, 128), wcol)
        return send(
            w_ref.at[:, :, cols],
            wg.at[:, pl.ds(pl.multiple_of(me * rows, rows), rows), cols],
            s_w.at[k], r_w.at[k], {"ctx": ctx_at(k)},
        )

    def g_copy(k, g):
        owner = lax.rem(me + n - k, n)
        piece = wg.at[
            :, pl.ds(pl.multiple_of(owner * rows, rows), rows), pl.ds(pl.multiple_of(my_gr * wcol, 128), wcol)
        ]
        return send(piece, piece, s_g.at[k, g], r_g.at[k, g], {"groups": gr_at(g)})

    for k in range(1, n):
        cot_copy(k).start()
    lower = (
        lax.broadcasted_iota(jnp.int32, (tokens, tokens), 0)
        >= lax.broadcasted_iota(jnp.int32, (tokens, tokens), 1)
    )
    tri = jnp.where(lower, 1.0, 0.0).astype(BF)

    def running(o, _):
        steps = steps_ref[o]
        high = (steps // 256).astype(F32).astype(BF)
        low = (steps % 256).astype(F32).astype(BF)
        runr[o] = dot(high, tri, 1, 1) * 256.0 + dot(low, tri, 1, 1)
        runc[o] = dot(tri, high, 1, 1) * 256.0 + dot(tri, low, 1, 1)
        return 0

    lax.fori_loop(0, 3, running, 0)

    def end_states(o, _):
        bt = wr_ref[o][:, :N]
        rc = runc[o] * scale
        falling = jnp.exp(rc[tokens - 1 :, :] - rc)
        for h in range(heads):
            xs = (x_ref[o, :, h * P_SIZE : (h + 1) * P_SIZE].astype(F32) * falling[:, h : h + 1]).astype(BF)
            ends[o, h] = dot(bt, xs, 0, 0)
        return 0

    lax.fori_loop(0, 3, end_states, 0)

    def end_copy(o):
        return send(ends_out.at[o], ends_in.at[o], s_end.at[o], r_end.at[o], {"ctx": lax.rem(me + 1, n)})

    def grad_copy(o):
        return send(grads_out.at[o], grads_in.at[o], s_gr.at[o], r_gr.at[o], {"ctx": lax.rem(me + n - 1, n)})

    def chain(o, copy_of, total, own, outgoing, incoming, first, last):
        @pl.when(jnp.logical_not(first))
        def _():
            copy_of(o).wait_recv()
            total[o] = incoming[o].astype(F32)

        @pl.when(jnp.logical_not(last))
        def _():
            fade = jnp.exp(runr[o][:, tokens - 1 :] * scale)
            for h in range(heads):
                outgoing[o, h] = (total[o, h] * fade[h : h + 1, :] + own[o, h]).astype(outgoing.dtype)
            copy_of(o).start()

    cotg[pl.ds(pl.multiple_of(me * blk, blk), blk), :] = cot_ref[pl.ds(pl.multiple_of(me * blk, blk), blk), :]
    wg[:, pl.ds(pl.multiple_of(me * rows, rows), rows), :] = w_ref[...]
    for k in range(1, n):
        cot_copy(k).wait()
    scanned[0] = cot_ref[...]

    def permute(o, _):
        ids = orders_ref[o]
        place = (ids // tokens) * blk + ids % blk
        hot = jnp.where(lax.broadcasted_iota(jnp.int32, (tokens, tokens), 0) == place, 1.0, 0.0).astype(BF)
        scanned[o + 1] = dot(hot, cotg[...], 0, 0).astype(BF)
        return 0

    lax.fori_loop(0, 2, permute, 0)

    state[...] = jnp.zeros_like(state)
    gout[...] = jnp.zeros_like(gout)
    def chain_one(o, _):
        chain(o, end_copy, state, ends, ends_out, ends_in, me == 0, me == n - 1)
        return 0

    lax.fori_loop(0, 3, chain_one, 0)

    for k in range(1, n):
        w_copy(k).start()
    def pair_copy(k, o):
        cols = pl.ds(pl.multiple_of((pair_at(k) - base_dp) * pcol, 128), pcol)
        return send(
            pb.at[o, :, cols], pa_in.at[k, o], s_a.at[k, o], r_a.at[k, o], {"dp": pair_at(k)}
        )

    def forward(o, _):
        bt = wr_ref[o][:, :N]
        ct = wr_ref[o][:, N:]
        scores = dot(ct, bt, 1, 1)
        rc = runc[o] * scale
        rr = runr[o] * scale
        rising = jnp.exp(rc)
        for h in range(heads):
            cut = slice(h * P_SIZE, (h + 1) * P_SIZE)
            decay = jnp.where(lower, jnp.exp(jnp.minimum(rc[:, h : h + 1] - rr[h : h + 1, :], 0.0)), 0.0)
            full = scores * decay
            mix = full.astype(BF)
            rest = (full - mix.astype(F32)).astype(BF)
            mixing[o, h] = mix
            up = (ct.astype(F32) * rising[:, h : h + 1]).astype(BF)
            outs[:, cut] = (
                dot(mix, x_ref[o, :, cut], 1, 0)
                + dot(rest, x_ref[o, :, cut], 1, 0)
                + dot(up, state[o, h].astype(BF), 1, 0)
            ).astype(BF)
        term = dot(scanned[o], outs[...], 0, 0)
        pf[o] = term
        pb[o] = term.astype(BF)
        for k in range(1, parts):
            pair_copy(k, o).start()
        return 0

    lax.fori_loop(0, 3, forward, 0)

    mine_cols = pl.ds(pl.multiple_of(my_part * pcol, 128), pcol)

    def ctx_copy(k, o):
        return send(
            sb.at[o, pl.ds(pl.multiple_of(ctx_at(k) * rows, rows), rows)],
            sb_in.at[k, o], s_b.at[k, o], r_b.at[k, o], {"ctx": ctx_at(k)},
        )

    def pair_sum(o, _):
        total = pf[o, :, mine_cols]
        for k in range(1, parts):
            pair_copy(k, o).wait()
            total = total + pa_in[k, o].astype(F32)
        pf[o, :, mine_cols] = total
        sb[o] = total.astype(BF)
        for k in range(1, n):
            ctx_copy(k, o).start()
        return 0

    for k in range(1, n):
        w_copy(k).wait()
        for g in range(1, n_gr):
            g_copy(k, g).start()
        if k == 1:
            pair_sum(0, 0)
    pair_sum(1, 0)
    for k in range(1, n):
        for g in range(1, n_gr):
            g_copy(k, g).wait()

    def upstream(o, _):
        ct = wr_ref[o][:, N:]
        dys[o] = dot(scanned[o], wg[o], 1, 0).astype(BF)
        rising = jnp.exp(runc[o] * scale)
        for h in range(heads):
            up = (ct.astype(F32) * rising[:, h : h + 1]).astype(BF)
            grads[o, h] = dot(up, dys[o, :, h * P_SIZE : (h + 1) * P_SIZE], 0, 0)
        return 0

    lax.fori_loop(0, 3, upstream, 0)
    pair_sum(2, 0)

    def dp_copy(k, o):
        return send(cb.at[o], cb_in.at[k, o], s_c.at[k, o], r_c.at[k, o], {"dp": dp_at(k)})

    def ctx_sum(o):
        total = pf[o, pl.ds(pl.multiple_of(me * rows, rows), rows), mine_cols]
        for k in range(1, n):
            ctx_copy(k, o).wait()
            total = total + sb_in[k, o].astype(F32)
        cb[o] = total.astype(BF)
        for k in range(1, n_dp):
            dp_copy(k, o).start()

    def backward(o, _):
        chain(o, grad_copy, gout, grads, grads_out, grads_in, me == n - 1, me == 0)
        bt = wr_ref[o][:, :N]
        ct = wr_ref[o][:, N:]
        rc = runc[o] * scale
        rr = runr[o] * scale
        rising = jnp.exp(rc)
        falling = jnp.exp(rc[tokens - 1 :, :] - rc)
        both = jnp.zeros((tokens, tokens), F32)
        gb = jnp.zeros((tokens, N), F32)
        gc = jnp.zeros((tokens, N), F32)
        for h in range(heads):
            cut = slice(h * P_SIZE, (h + 1) * P_SIZE)
            xs = x_ref[o, :, cut]
            dy = dys[o, :, cut]
            far = gout[o, h].astype(BF)
            down = (bt.astype(F32) * falling[:, h : h + 1]).astype(BF)
            gx_ref[o, :, cut] = (dot(mixing[o, h], dy, 0, 0) + dot(down, far, 1, 0)).astype(BF)
            decay = jnp.where(lower, jnp.exp(jnp.minimum(rc[:, h : h + 1] - rr[h : h + 1, :], 0.0)), 0.0)
            both = both + dot(dy, xs, 1, 1) * decay
            gb = gb + falling[:, h : h + 1] * dot(xs, far, 1, 1)
            gc = gc + rising[:, h : h + 1] * dot(dy, state[o, h].astype(BF), 1, 1)
        both = both.astype(BF)
        part[o, :, :N] = gb + dot(both, ct, 0, 0)
        part[o, :, N:] = gc + dot(both, bt, 1, 0)

        @pl.when(o < 2)
        def _():
            ctx_sum(o)

        return 0

    lax.fori_loop(0, 3, backward, 0)

    def mp_copy(k):
        return send(part, part_in.at[k], s_m.at[k], r_m.at[k], {"mp": lax.rem(my_mp + k, n_mp)})

    for k in range(1, n_mp):
        mp_copy(k).start()

    ctx_sum(2)
    for k in range(1, n_mp):
        mp_copy(k).wait()
    total = part[...]
    for k in range(1, n_mp):
        total = total + part_in[k]
    gwr_ref[...] = total.astype(BF)
    for k in range(1, n_dp):
        for o in range(3):
            dp_copy(k, o).wait()
    for u in range(parts):
        sum_u = jnp.zeros((3, rows, pcol), F32)
        own = cb[...].astype(F32)
        for k in range(n_dp):
            piece = own if k == 0 else cb_in[k].astype(F32)
            belongs = lax.rem(my_dp + n_dp - k, parts) == u
            sum_u = sum_u + jnp.where(belongs, piece, 0.0)
        gw_ref[:, :, u * pcol : (u + 1) * pcol] = sum_u.astype(BF)

    for o in range(3):

        @pl.when(me < n - 1)
        def _():
            end_copy(o).wait_send()

        @pl.when(me > 0)
        def _():
            grad_copy(o).wait_send()


def shards(sizes, head_inputs, write_read, decay_steps, scan_orders, cotangent, out_weight):
    n, n_dp, n_gr, n_mp = sizes
    tokens, width = cotangent.shape[1:]
    inner = head_inputs.shape[3]
    heads = decay_steps.shape[2]
    rows = out_weight.shape[1]
    parts = math.gcd(inner // 128, n_dp)
    pcol = inner // parts
    x = head_inputs.reshape(3, tokens, inner)
    wr = write_read.reshape(3, tokens, 2 * N)
    steps = jnp.pad(decay_steps.reshape(3, heads, tokens), ((0, 0), (0, -heads % 8), (0, 0)))
    hp = steps.shape[1]
    chained = BF if n <= 4 else F32
    V = pltpu.VMEM
    dma = pltpu.SemaphoreType.DMA
    scratch = [
        V((tokens, width), BF), V((3, width, inner), BF),
        *[V((3, heads, N, P_SIZE), kind) for kind in (F32, chained, chained, F32)] * 2,
        V((3, tokens, width), BF), V((3, heads, tokens, tokens), BF), V((tokens, inner), BF),
        V((3, tokens, inner), BF),
        V((3, width, inner), F32), V((3, width, inner), BF), V((parts, 3, width, pcol), BF),
        V((3, width, pcol), BF), V((n, 3, rows, pcol), BF), V((3, rows, pcol), BF), V((n_dp, 3, rows, pcol), BF),
        V((3, tokens, hp), F32), V((3, hp, tokens), F32),
        V((3, tokens, 2 * N), F32), V((n_mp, 3, tokens, 2 * N), F32),
        dma((n,)), dma((n,)), dma((n,)), dma((n,)), dma((n, n_gr)), dma((n, n_gr)),
        dma((3,)), dma((3,)), dma((3,)), dma((3,)), dma((parts, 3)), dma((parts, 3)), dma((n, 3)), dma((n, 3)),
        dma((n_dp, 3)), dma((n_dp, 3)), dma((n_mp,)), dma((n_mp,)),
    ]
    gx, gwr, gw = pl.pallas_call(
        functools.partial(kernel, sizes),
        out_shape=(
            jax.ShapeDtypeStruct((3, tokens, inner), BF),
            jax.ShapeDtypeStruct((3, tokens, 2 * N), BF),
            jax.ShapeDtypeStruct((3, rows, inner), BF),
        ),
        in_specs=[pl.BlockSpec(memory_space=V)] * 6,
        out_specs=(pl.BlockSpec(memory_space=V),) * 3,
        scratch_shapes=scratch,
        compiler_params=pltpu.CompilerParams(
            collective_id=0, has_side_effects=True, vmem_limit_bytes=60 * 2**20
        ),
    )(x, wr, steps, scan_orders.reshape(2, 1, tokens), cotangent.reshape(tokens, width), out_weight)
    return gx[:, None], gwr[:, None], gw


def solution(mesh):
    sizes = (mesh.shape["ctx"], mesh.shape["dp"], mesh.shape["groups"], mesh.shape["mp"])
    in_specs = (
        P(None, ("groups", "dp"), "ctx", "mp"),
        P(None, ("groups", "dp"), "ctx", None),
        P(None, ("groups", "dp"), "mp", "ctx"),
        P(None, ("groups", "dp"), "ctx"),
        P(("groups", "dp"), "ctx", None),
        P(None, "ctx", "mp"),
    )
    out_specs = (
        P(None, ("groups", "dp"), "ctx", "mp"),
        P(None, ("groups", "dp"), "ctx", None),
        P("groups", "ctx", "mp"),
    )
    return jax.shard_map(
        functools.partial(shards, sizes), mesh=mesh, in_specs=in_specs, out_specs=out_specs, check_vma=False
    )
```
